512 devices in a mesh: energy: 64 (over x, z), slab: 8 (over y, core).
Axes of the slice: x: 4, y: 4, z: 16, core: 2. Of those that a mesh axis runs over, the one named last changes fastest.
Arguments:
- green_block: bfloat16 [64, 8, 2, 192, 192], P('energy', 'slab'), may hold values from -0.4375 to 0.4375
- coupling: bfloat16 [64, 8, 2, 192, 192], P('energy', 'slab'), may hold values from -0.4375 to 0.4375
- sigma_lesser: bfloat16 [64, 8, 2, 192, 192], P('energy', 'slab'), may hold values from -6 to 6
- screened: bfloat16 [8, 2, 128, 36864], P('slab', None, None, 'energy'), may hold values from -9 to 9
Outputs:
- sigma_next: bfloat16 [64, 8, 2, 192, 192], P('energy', 'slab')
The draws below stay inside these ranges and needn't reach their ends.
All inputs are finite; a program needn't handle non-finite values.
Results may differ from the reference program's by a relative error of at most 0.0049.
Values may be sent and summed in bfloat16 or wider, within the bound.
No kernel may reach another device: no remote copies, remote signals or barrier semaphores. Data moves between devices by JAX's collectives and lax.ppermute only.
A program may use at most 128 MiB of HBM per device.

```python
import math
import jax
import jax.numpy as jnp
from jax import lax

M = 192
BLOCKS = 8
ENERGIES = 64
FREQ = 128
PAIRS = 36864


def block_scale(rng, dims, pieces, least, largest):
    gain, own = 1.0, jax.random.fold_in(rng, 6)
    for dim, blocks in pieces:
        draws = jnp.exp(jax.random.uniform(jax.random.fold_in(own, dim), (blocks,), jnp.float32, least / len(pieces), largest / len(pieces)))
        gain = gain * jnp.repeat(draws, dims[dim] // blocks).reshape([-1 if axis == dim else 1 for axis in range(len(dims))])
    return gain


def noise(rng, dims, scale, reach, split=(), kind=jnp.bfloat16):
    drawn = jax.random.normal(rng, dims, jnp.float32) * scale
    if len(split) > 0:
        drawn = block_scale(rng, dims, split, -0.22, 0.18) * drawn
    return jnp.clip(drawn, min=-reach, max=reach).astype(kind)


def setup_inputs(seed: int = 0) -> dict:
    key_list = jax.random.split(jax.random.key(seed), 5)
    green_block = noise(key_list[0], (ENERGIES, BLOCKS, 2, M, M), M ** -0.5, 0.4375, ((0, 64), (1, 8)))
    coupling = noise(key_list[1], (ENERGIES, BLOCKS, 2, M, M), M ** -0.5, 0.4375, ((0, 64), (1, 8)))
    sigma_lesser = noise(key_list[2], (ENERGIES, BLOCKS, 2, M, M), 1.0, 6.0, ((0, 64), (1, 8)))
    screened = noise(key_list[3], (BLOCKS, 2, FREQ, PAIRS), 1.5, 9.0, ((0, 8), (3, 64)))
    return {"green_block": green_block, "coupling": coupling, "sigma_lesser": sigma_lesser, "screened": screened}


def sandwich(outer, inner):
    outer_real = outer[:, 0].astype(jnp.float32)
    outer_imag = outer[:, 1].astype(jnp.float32)
    inner_real = inner[:, 0].astype(jnp.float32)
    inner_imag = inner[:, 1].astype(jnp.float32)
    forward = "eij,ejk->eik"
    adjoint = "eik,ejk->eij"
    half_real = jnp.einsum(forward, outer_real, inner_real) - jnp.einsum(forward, outer_imag, inner_imag)
    half_imag = jnp.einsum(forward, outer_real, inner_imag) + jnp.einsum(forward, outer_imag, inner_real)
    half_real = lax.optimization_barrier(half_real.astype(jnp.bfloat16)).astype(jnp.float32)
    half_imag = lax.optimization_barrier(half_imag.astype(jnp.bfloat16)).astype(jnp.float32)
    full_real = jnp.einsum(adjoint, half_real, outer_real) + jnp.einsum(adjoint, half_imag, outer_imag)
    full_imag = jnp.einsum(adjoint, half_imag, outer_real) - jnp.einsum(adjoint, half_real, outer_imag)
    return full_real, full_imag


def tables(count):
    length = 2 * count
    rows = jnp.arange(length, dtype=jnp.int32)
    cols = jnp.arange(count, dtype=jnp.int32)
    phases = (rows[:, None] * cols[None, :]) % length
    angles = phases.astype(jnp.float32) * (2.0 * math.pi / length)
    return jnp.cos(angles), jnp.sin(angles)


def reference(green_block, coupling, sigma_lesser, screened):
    high = lax.Precision.HIGHEST
    cosine, sine = tables(ENERGIES)
    results = []
    for position in range(BLOCKS):
        half_own_real, half_own_imag = sandwich(green_block[:, position], sigma_lesser[:, position])
        lesser_real, lesser_imag = half_own_real, half_own_imag
        if position + 1 < BLOCKS:
            half_next_real, half_next_imag = sandwich(coupling[:, position], sigma_lesser[:, position + 1])
            lesser_real = lesser_real + half_next_real
            lesser_imag = lesser_imag + half_next_imag
        flat_real = lesser_real.reshape(ENERGIES, PAIRS)
        flat_imag = lesser_imag.reshape(ENERGIES, PAIRS)
        spec_real = jnp.dot(cosine, flat_real, precision=high) + jnp.dot(sine, flat_imag, precision=high)
        spec_imag = jnp.dot(cosine, flat_imag, precision=high) - jnp.dot(sine, flat_real, precision=high)
        screen_real = screened[position, 0].astype(jnp.float32)
        screen_imag = screened[position, 1].astype(jnp.float32)
        conv_real = spec_real * screen_real - spec_imag * screen_imag
        conv_imag = spec_real * screen_imag + spec_imag * screen_real
        back_real = jnp.dot(cosine.T, conv_real, precision=high) - jnp.dot(sine.T, conv_imag, precision=high)
        back_imag = jnp.dot(cosine.T, conv_imag, precision=high) + jnp.dot(sine.T, conv_real, precision=high)
        joined = jnp.stack([back_real, back_imag], axis=1) / FREQ
        results.append(joined.reshape(ENERGIES, 2, M, M).astype(jnp.bfloat16))
    return jnp.stack(results, axis=1)
```

```python
import math

import jax
import jax.numpy as jnp
import numpy as np
from jax import lax
from jax.experimental import pallas as pl
from jax.experimental.pallas import tpu as pltpu
from jax.sharding import PartitionSpec as P

M = 192
OWNERS = 64
ROWS = M // OWNERS
WIDTH = ROWS * M
FREQ = 128
LANES = 128


def dot(first, second):
    return jnp.dot(first, second, preferred_element_type=jnp.float32)


def dot_t(first, second):
    return lax.dot_general(first, second, (((1,), (1,)), ((), ())), preferred_element_type=jnp.float32)


def put(ref, where, value):
    for lane in range(0, value.shape[1], LANES):
        piece = value[:, lane : lane + LANES]
        ref[lane // LANES, where, : piece.shape[1]] = piece


def term(outer, inner, half, left, right):
    outer_real, outer_imag = outer[0, 0, 0], outer[0, 0, 1]
    inner_real, inner_imag = inner[0, 0, 0], inner[0, 0, 1]
    half_real = dot(outer_real, inner_real) - dot(outer_imag, inner_imag)
    half_imag = dot(outer_real, inner_imag) + dot(outer_imag, inner_real)
    put(half, slice(0, M), half_real.astype(jnp.bfloat16).astype(jnp.float32))
    put(half, slice(M, 2 * M), half_imag.astype(jnp.bfloat16).astype(jnp.float32))
    for plane in range(2):
        for row in range(ROWS):
            real = half[plane, pl.ds(row, OWNERS, stride=ROWS), :]
            imag = half[plane, pl.ds(M + row, OWNERS, stride=ROWS), :]
            first = 2 * OWNERS * row
            left[plane, pl.ds(first, OWNERS, stride=2), :] = real
            left[plane, pl.ds(first + 1, OWNERS, stride=2), :] = imag
            right[plane, pl.ds(first, OWNERS, stride=2), :] = imag
            right[plane, pl.ds(first + 1, OWNERS, stride=2), :] = -real
    left_all = jnp.concatenate([left[0], left[1, :, : M - LANES]], axis=1).astype(jnp.bfloat16)
    right_all = jnp.concatenate([right[0], right[1, :, : M - LANES]], axis=1).astype(jnp.bfloat16)
    full = dot_t(left_all, outer_real) + dot_t(right_all, outer_imag)
    return jnp.concatenate([full[2 * OWNERS * row : 2 * OWNERS * (row + 1)] for row in range(ROWS)], axis=1)


def own_kernel(green, sigma, out, half, left, right):
    out[...] = term(green, sigma, half, left, right)


def next_kernel(coupling, sigma, own, out, half, left, right):
    out[...] = (own[...] + term(coupling, sigma, half, left, right)).astype(jnp.bfloat16)


def convolve_kernel(columns, screened, forward, backward, out):
    value = columns[...]
    spectrum = dot(forward[...], jnp.concatenate([value, value], axis=0))
    spec_real, spec_imag = spectrum[:FREQ], spectrum[FREQ:]
    screen_real = screened[0, 0].astype(jnp.float32)
    screen_imag = screened[0, 1].astype(jnp.float32)
    conv_real = spec_real * screen_real - spec_imag * screen_imag
    conv_imag = spec_real * screen_imag + spec_imag * screen_real
    conv = jnp.concatenate([conv_real, conv_imag], axis=0)
    high = conv.astype(jnp.bfloat16)
    low = (conv - high.astype(jnp.float32)).astype(jnp.bfloat16)
    out[...] = dot(backward[...], jnp.concatenate([high, high, low], axis=0)).astype(jnp.bfloat16)


def unpack_kernel(packed, out, flat, rows):
    put(flat, slice(0, 2 * OWNERS), packed[...].astype(jnp.float32))
    planes = flat.shape[0]
    for part in range(2):
        both = jnp.concatenate([flat[plane, pl.ds(part, OWNERS, stride=2), :] for plane in range(planes)], axis=1)
        for row in range(ROWS):
            value = both[:, M * row : M * (row + 1)]
            put(rows, pl.ds(M * part + row, OWNERS, stride=ROWS), value)
        every = slice(M * part, M * (part + 1))
        out[0, 0, part, :, :LANES] = rows[0, every, :].astype(jnp.bfloat16)
        out[0, 0, part, :, LANES:] = rows[1, every, : M - LANES].astype(jnp.bfloat16)


def split(table):
    high = table.astype(jnp.bfloat16)
    low = (table - high.astype(np.float64)).astype(jnp.bfloat16)
    return high, low


def tables():
    phases = np.outer(np.arange(FREQ), np.arange(OWNERS)) % FREQ
    angles = phases * (2.0 * math.pi / FREQ)
    cosine, sine = np.cos(angles), np.sin(angles)
    from_real = np.concatenate([cosine, -sine], axis=0)
    from_imag = np.concatenate([sine, cosine], axis=0)
    forward = np.stack([from_real, from_imag], axis=-1).reshape(2 * FREQ, 2 * OWNERS)
    to_real = np.concatenate([cosine.T, -sine.T], axis=1)
    to_imag = np.concatenate([sine.T, cosine.T], axis=1)
    backward = np.stack([to_real, to_imag], axis=1).reshape(2 * OWNERS, 2 * FREQ) / FREQ
    forward_high, forward_low = split(forward)
    back_high, back_low = split(backward)
    return (
        np.concatenate([forward_high, forward_low], axis=1),
        np.concatenate([back_high, back_low, back_high], axis=1),
    )


def call(kernel, shape, dtype, scratch, flops, moved, *values):
    vmem = pl.BlockSpec(memory_space=pltpu.VMEM)
    return pl.pallas_call(
        kernel,
        out_shape=jax.ShapeDtypeStruct(shape, dtype),
        in_specs=[vmem] * len(values),
        out_specs=vmem,
        scratch_shapes=scratch,
        compiler_params=pltpu.CompilerParams(vmem_limit_bytes=24 * 2**20),
        cost_estimate=pl.CostEstimate(flops=flops, bytes_accessed=moved, transcendentals=0),
    )(*values)


def shards(green_block, coupling, sigma_lesser, screened):
    count = lax.axis_size("slab")
    sigma_next = lax.ppermute(sigma_lesser, "slab", [(place + 1, place) for place in range(count - 1)])
    scratch = [
        pltpu.VMEM((2, 2 * M, LANES), jnp.float32),
        pltpu.VMEM((2, 2 * M, LANES), jnp.float32),
        pltpu.VMEM((2, 2 * M, LANES), jnp.float32),
    ]
    packed = (2 * OWNERS, WIDTH)
    flops = 16 * M**3
    own = call(own_kernel, packed, jnp.float32, scratch, flops, 600000, green_block, sigma_lesser)
    lesser = call(next_kernel, packed, jnp.bfloat16, scratch, flops, 700000, coupling, sigma_next, own)
    columns = lax.all_to_all(lesser.reshape(OWNERS, 2, WIDTH), "energy", split_axis=0, concat_axis=0, tiled=True)
    forward, backward = tables()
    back = call(
        convolve_kernel, packed, jnp.bfloat16, [], 2 * 5 * 256 * 128 * WIDTH, 800000,
        columns.reshape(packed), screened, jnp.asarray(forward), jnp.asarray(backward),
    )
    returned = lax.all_to_all(back.reshape(OWNERS, 2, WIDTH), "energy", split_axis=0, concat_axis=0, tiled=True)
    return call(
        unpack_kernel, (1, 1, 2, M, M), jnp.bfloat16,
        [pltpu.VMEM((5, 2 * OWNERS, LANES), jnp.float32), pltpu.VMEM((2, 2 * M, LANES), jnp.float32)],
        1000000, 300000, returned.reshape(packed),
    )


def solution(mesh):
    placed = (
        P("energy", "slab", None, None, None),
        P("energy", "slab", None, None, None),
        P("energy", "slab", None, None, None),
        P("slab", None, None, "energy"),
    )
    return jax.shard_map(
        shards,
        mesh=mesh,
        in_specs=placed,
        out_specs=P("energy", "slab", None, None, None),
        check_vma=False,
    )
```

```python
import math

import jax
import jax.numpy as jnp
import numpy as np
from jax import lax
from jax.experimental import pallas as pl
from jax.experimental.pallas import tpu as pltpu
from jax.sharding import PartitionSpec as P

M = 192
OWNERS = 64
ROWS = M // OWNERS
WIDTH = ROWS * M
FREQ = 128
LANES = 128


def dot(first, second):
    return jnp.dot(first, second, preferred_element_type=jnp.float32)


def dot_t(first, second):
    return lax.dot_general(first, second, (((1,), (1,)), ((), ())), preferred_element_type=jnp.float32)


def put(ref, where, value):
    for lane in range(0, value.shape[1], LANES):
        piece = value[:, lane : lane + LANES]
        ref[lane // LANES, where, : piece.shape[1]] = piece


def term(outer, inner, half, left, right):
    outer_real, outer_imag = outer[0, 0, 0], outer[0, 0, 1]
    inner_real, inner_imag = inner[0, 0, 0], inner[0, 0, 1]
    half_real = dot(outer_real, inner_real) - dot(outer_imag, inner_imag)
    half_imag = dot(outer_real, inner_imag) + dot(outer_imag, inner_real)
    put(half, slice(0, M), half_real.astype(jnp.bfloat16).astype(jnp.float32))
    put(half, slice(M, 2 * M), half_imag.astype(jnp.bfloat16).astype(jnp.float32))
    for plane in range(2):
        for row in range(ROWS):
            real = half[plane, pl.ds(row, OWNERS, stride=ROWS), :]
            imag = half[plane, pl.ds(M + row, OWNERS, stride=ROWS), :]
            first = 2 * OWNERS * row
            left[plane, pl.ds(first, OWNERS, stride=2), :] = real
            left[plane, pl.ds(first + 1, OWNERS, stride=2), :] = imag
            right[plane, pl.ds(first, OWNERS, stride=2), :] = imag
            right[plane, pl.ds(first + 1, OWNERS, stride=2), :] = -real
    left_all = jnp.concatenate([left[0], left[1, :, : M - LANES]], axis=1).astype(jnp.bfloat16)
    right_all = jnp.concatenate([right[0], right[1, :, : M - LANES]], axis=1).astype(jnp.bfloat16)
    full = dot_t(left_all, outer_real) + dot_t(right_all, outer_imag)
    return jnp.concatenate([full[2 * OWNERS * row : 2 * OWNERS * (row + 1)] for row in range(ROWS)], axis=1)


def own_kernel(green, sigma, out, half, left, right):
    out[...] = term(green, sigma, half, left, right)


def next_kernel(coupling, sigma, own, out, half, left, right):
    inside = lax.axis_index("slab") < lax.axis_size("slab") - 1
    added = jnp.where(inside, term(coupling, sigma, half, left, right), 0.0)
    out[...] = (own[...] + added).astype(jnp.bfloat16).reshape(out.shape)


def convolve_kernel(columns, screened, forward, backward, out):
    value = columns[...].reshape(2 * OWNERS, WIDTH)
    spectrum = dot(forward[...], jnp.concatenate([value, value], axis=0))
    spec_real, spec_imag = spectrum[:FREQ], spectrum[FREQ:]
    screen_real = screened[0, 0].astype(jnp.float32)
    screen_imag = screened[0, 1].astype(jnp.float32)
    conv_real = spec_real * screen_real - spec_imag * screen_imag
    conv_imag = spec_real * screen_imag + spec_imag * screen_real
    conv = jnp.concatenate([conv_real, conv_imag], axis=0)
    high = conv.astype(jnp.bfloat16)
    low = (conv - high.astype(jnp.float32)).astype(jnp.bfloat16)
    out[...] = dot(backward[...], jnp.concatenate([high, high, low], axis=0)).astype(jnp.bfloat16).reshape(out.shape)


def unpack_kernel(packed, out, flat, rows, near, sems):
    put(flat, slice(0, 2 * OWNERS), packed[...].reshape(2 * OWNERS, WIDTH).astype(jnp.float32))
    planes = flat.shape[0]
    copies = [pltpu.make_async_copy(near.at[part], out.at[0, 0, part], sems.at[part]) for part in range(2)]
    for part in range(2):
        both = jnp.concatenate([flat[plane, pl.ds(part, OWNERS, stride=2), :] for plane in range(planes)], axis=1)
        for row in range(ROWS):
            value = both[:, M * row : M * (row + 1)]
            put(rows, pl.ds(M * part + row, OWNERS, stride=ROWS), value)
        every = slice(M * part, M * (part + 1))
        near[part, :, :LANES] = rows[0, every, :].astype(jnp.bfloat16)
        near[part, :, LANES:] = rows[1, every, : M - LANES].astype(jnp.bfloat16)
        copies[part].start()
    for copy in copies:
        copy.wait()


def split(table):
    high = table.astype(jnp.bfloat16)
    low = (table - high.astype(np.float64)).astype(jnp.bfloat16)
    return high, low


def tables():
    phases = np.outer(np.arange(FREQ), np.arange(OWNERS)) % FREQ
    angles = phases * (2.0 * math.pi / FREQ)
    cosine, sine = np.cos(angles), np.sin(angles)
    from_real = np.concatenate([cosine, -sine], axis=0)
    from_imag = np.concatenate([sine, cosine], axis=0)
    forward = np.stack([from_real, from_imag], axis=-1).reshape(2 * FREQ, 2 * OWNERS)
    to_real = np.concatenate([cosine.T, -sine.T], axis=1)
    to_imag = np.concatenate([sine.T, cosine.T], axis=1)
    backward = np.stack([to_real, to_imag], axis=1).reshape(2 * OWNERS, 2 * FREQ) / FREQ
    forward_high, forward_low = split(forward)
    back_high, back_low = split(backward)
    return (
        np.concatenate([forward_high, forward_low], axis=1),
        np.concatenate([back_high, back_low, back_high], axis=1),
    )


def call(kernel, shape, dtype, scratch, flops, moved, *values, far=False):
    vmem = pl.BlockSpec(memory_space=pltpu.VMEM)
    return pl.pallas_call(
        kernel,
        out_shape=jax.ShapeDtypeStruct(shape, dtype),
        in_specs=[vmem] * len(values),
        out_specs=pl.BlockSpec(memory_space=pl.ANY) if far else vmem,
        scratch_shapes=scratch,
        compiler_params=pltpu.CompilerParams(vmem_limit_bytes=24 * 2**20),
        cost_estimate=pl.CostEstimate(flops=flops, bytes_accessed=moved, transcendentals=0),
    )(*values)


def shards(green_block, coupling, sigma_lesser, screened):
    count = lax.axis_size("slab")
    sigma_next = lax.ppermute(sigma_lesser, "slab", [((place + 1) % count, place) for place in range(count)])
    scratch = [
        pltpu.VMEM((2, 2 * M, LANES), jnp.float32),
        pltpu.VMEM((2, 2 * M, LANES), jnp.float32),
        pltpu.VMEM((2, 2 * M, LANES), jnp.float32),
    ]
    packed = (OWNERS, 2, WIDTH)
    flops = 16 * M**3
    own = call(own_kernel, (2 * OWNERS, WIDTH), jnp.float32, scratch, flops, 600000, green_block, sigma_lesser)
    lesser = call(next_kernel, packed, jnp.bfloat16, scratch, flops, 700000, coupling, sigma_next, own)
    columns = lax.all_to_all(lesser, "energy", split_axis=0, concat_axis=0, tiled=True)
    forward, backward = tables()
    back = call(
        convolve_kernel, packed, jnp.bfloat16, [], 2 * 5 * 256 * 128 * WIDTH, 800000,
        columns, screened, jnp.asarray(forward), jnp.asarray(backward),
    )
    returned = lax.all_to_all(back, "energy", split_axis=0, concat_axis=0, tiled=True)
    return call(
        unpack_kernel, (1, 1, 2, M, M), jnp.bfloat16,
        [
            pltpu.VMEM((5, 2 * OWNERS, LANES), jnp.float32),
            pltpu.VMEM((2, 2 * M, LANES), jnp.float32),
            pltpu.VMEM((2, M, M), jnp.bfloat16),
            pltpu.SemaphoreType.DMA((2,)),
        ],
        1000000, 300000, returned, far=True,
    )


def solution(mesh):
    placed = (
        P("energy", "slab", None, None, None),
        P("energy", "slab", None, None, None),
        P("energy", "slab", None, None, None),
        P("slab", None, None, "energy"),
    )
    return jax.shard_map(
        shards,
        mesh=mesh,
        in_specs=placed,
        out_specs=P("energy", "slab", None, None, None),
        check_vma=False,
    )
```

```python
import math

import jax
import jax.numpy as jnp
import numpy as np
from jax import lax
from jax.experimental import pallas as pl
from jax.experimental.pallas import tpu as pltpu
from jax.sharding import PartitionSpec as P

M = 192
OWNERS = 64
ROWS = M // OWNERS
WIDTH = ROWS * M
FREQ = 128
LANES = 128


def dot(first, second):
    return jnp.dot(first, second, preferred_element_type=jnp.float32)


def dot_t(first, second):
    return lax.dot_general(first, second, (((1,), (1,)), ((), ())), preferred_element_type=jnp.float32)


def put(ref, where, value):
    for lane in range(0, value.shape[1], LANES):
        piece = value[:, lane : lane + LANES]
        ref[lane // LANES, where, : piece.shape[1]] = piece


def term(outer, inner, half, left, right):
    outer_real, outer_imag = outer[0, 0, 0], outer[0, 0, 1]
    inner_real, inner_imag = inner[0, 0, 0], inner[0, 0, 1]
    half_real = dot(outer_real, inner_real) - dot(outer_imag, inner_imag)
    half_imag = dot(outer_real, inner_imag) + dot(outer_imag, inner_real)
    put(half, slice(0, M), half_real.astype(jnp.bfloat16).astype(jnp.float32))
    put(half, slice(M, 2 * M), half_imag.astype(jnp.bfloat16).astype(jnp.float32))
    for plane in range(2):
        for row in range(ROWS):
            real = half[plane, pl.ds(row, OWNERS, stride=ROWS), :]
            imag = half[plane, pl.ds(M + row, OWNERS, stride=ROWS), :]
            first = 2 * OWNERS * row
            left[plane, pl.ds(first, OWNERS, stride=2), :] = real
            left[plane, pl.ds(first + 1, OWNERS, stride=2), :] = imag
            right[plane, pl.ds(first, OWNERS, stride=2), :] = imag
            right[plane, pl.ds(first + 1, OWNERS, stride=2), :] = -real
    left_all = jnp.concatenate([left[0], left[1, :, : M - LANES]], axis=1).astype(jnp.bfloat16)
    right_all = jnp.concatenate([right[0], right[1, :, : M - LANES]], axis=1).astype(jnp.bfloat16)
    full = dot_t(left_all, outer_real) + dot_t(right_all, outer_imag)
    return jnp.concatenate([full[2 * OWNERS * row : 2 * OWNERS * (row + 1)] for row in range(ROWS)], axis=1)


def own_kernel(green, sigma, out, half, left, right):
    out[...] = term(green, sigma, half, left, right)


def next_kernel(coupling, sigma, own, out, half, left, right):
    inside = lax.axis_index("slab") < lax.axis_size("slab") - 1
    added = jnp.where(inside, term(coupling, sigma, half, left, right), 0.0)
    out[...] = (own[...] + added).astype(jnp.bfloat16).reshape(out.shape)


def prepare_kernel(screened, forward, backward, turned, forward_out, backward_out):
    for part in range(2):
        turned[part] = screened[0, part].T
    forward_out[...] = forward[...]
    backward_out[...] = backward[...]


def convolve_kernel(columns, screened, forward, backward, out):
    value = columns[...].reshape(2 * OWNERS, WIDTH)
    spectrum = dot(forward[...], jnp.concatenate([value, value], axis=0))
    spec_real, spec_imag = spectrum[:FREQ], spectrum[FREQ:]
    screen_real = screened[0].astype(jnp.float32)
    screen_imag = screened[1].astype(jnp.float32)
    conv_real = spec_real * screen_real - spec_imag * screen_imag
    conv_imag = spec_real * screen_imag + spec_imag * screen_real
    conv = jnp.concatenate([conv_real, conv_imag], axis=0)
    high = conv.astype(jnp.bfloat16)
    low = (conv - high.astype(jnp.float32)).astype(jnp.bfloat16)
    out[...] = dot(backward[...], jnp.concatenate([high, high, low], axis=0)).astype(jnp.bfloat16).reshape(out.shape)


def unpack_kernel(packed, out, flat, rows, near, sems):
    put(flat, slice(0, 2 * OWNERS), packed[...].reshape(2 * OWNERS, WIDTH).astype(jnp.float32))
    planes = flat.shape[0]
    copies = [pltpu.make_async_copy(near.at[part], out.at[0, 0, part], sems.at[part]) for part in range(2)]
    for part in range(2):
        both = jnp.concatenate([flat[plane, pl.ds(part, OWNERS, stride=2), :] for plane in range(planes)], axis=1)
        for row in range(ROWS):
            value = both[:, M * row : M * (row + 1)]
            put(rows, pl.ds(M * part + row, OWNERS, stride=ROWS), value)
        every = slice(M * part, M * (part + 1))
        near[part, :, :LANES] = rows[0, every, :].astype(jnp.bfloat16)
        near[part, :, LANES:] = rows[1, every, : M - LANES].astype(jnp.bfloat16)
        copies[part].start()
    for copy in copies:
        copy.wait()


def split(table):
    high = table.astype(jnp.bfloat16)
    low = (table - high.astype(np.float64)).astype(jnp.bfloat16)
    return high, low


def tables():
    phases = np.outer(np.arange(FREQ), np.arange(OWNERS)) % FREQ
    angles = phases * (2.0 * math.pi / FREQ)
    cosine, sine = np.cos(angles), np.sin(angles)
    from_real = np.concatenate([cosine, -sine], axis=0)
    from_imag = np.concatenate([sine, cosine], axis=0)
    forward = np.stack([from_real, from_imag], axis=-1).reshape(2 * FREQ, 2 * OWNERS)
    to_real = np.concatenate([cosine.T, -sine.T], axis=1)
    to_imag = np.concatenate([sine.T, cosine.T], axis=1)
    backward = np.stack([to_real, to_imag], axis=1).reshape(2 * OWNERS, 2 * FREQ) / FREQ
    forward_high, forward_low = split(forward)
    back_high, back_low = split(backward)
    return (
        np.concatenate([forward_high, forward_low], axis=1),
        np.concatenate([back_high, back_low, back_high], axis=1),
    )


def shaped(shape, dtype=jnp.bfloat16):
    return jax.ShapeDtypeStruct(shape, dtype)


def call(kernel, shapes, flops, moved, *values, scratch=(), far=False):
    vmem = pl.BlockSpec(memory_space=pltpu.VMEM)
    return pl.pallas_call(
        kernel,
        out_shape=shapes,
        in_specs=[vmem] * len(values),
        out_specs=[pl.BlockSpec(memory_space=pl.ANY) if far else vmem] * len(shapes),
        scratch_shapes=scratch,
        compiler_params=pltpu.CompilerParams(vmem_limit_bytes=24 * 2**20),
        cost_estimate=pl.CostEstimate(flops=flops, bytes_accessed=moved, transcendentals=0),
    )(*values)


def shards(green_block, coupling, sigma_lesser, screened):
    count = lax.axis_size("slab")
    sigma_next = lax.ppermute(sigma_lesser, "slab", [((place + 1) % count, place) for place in range(count)])
    planes = [pltpu.VMEM((2, 2 * M, LANES), jnp.float32)] * 3
    packed = shaped((OWNERS, 2, WIDTH))
    flops = 16 * M**3
    (own,) = call(own_kernel, [shaped((2 * OWNERS, WIDTH), jnp.float32)], flops, 600000, green_block, sigma_lesser, scratch=planes)
    forward, backward = tables()
    turned, forward, backward = call(
        prepare_kernel, [shaped((2, FREQ, WIDTH)), shaped(forward.shape), shaped(backward.shape)], flops, 1200000,
        screened.transpose(0, 1, 3, 2), jnp.asarray(forward), jnp.asarray(backward),
    )
    own, turned, forward, backward = lax.optimization_barrier((own, turned, forward, backward))
    (lesser,) = call(next_kernel, [packed], flops, 700000, coupling, sigma_next, own, scratch=planes)
    columns = lax.all_to_all(lesser, "energy", split_axis=0, concat_axis=0, tiled=True)
    (joined,) = call(convolve_kernel, [packed], 2 * 5 * 256 * 128 * WIDTH, 800000, columns, turned, forward, backward)
    returned = lax.all_to_all(joined, "energy", split_axis=0, concat_axis=0, tiled=True)
    (result,) = call(
        unpack_kernel, [shaped(sigma_lesser.shape)], 1000000, 300000, returned,
        scratch=[
            pltpu.VMEM((5, 2 * OWNERS, LANES), jnp.float32),
            pltpu.VMEM((2, 2 * M, LANES), jnp.float32),
            pltpu.VMEM((2, M, M), jnp.bfloat16),
            pltpu.SemaphoreType.DMA((2,)),
        ],
        far=True,
    )
    return result


def solution(mesh):
    placed = (
        P("energy", "slab", None, None, None),
        P("energy", "slab", None, None, None),
        P("energy", "slab", None, None, None),
        P("slab", None, None, "energy"),
    )
    return jax.shard_map(
        shards,
        mesh=mesh,
        in_specs=placed,
        out_specs=P("energy", "slab", None, None, None),
        check_vma=False,
    )
```

```python
import math

import jax
import jax.numpy as jnp
import numpy as np
from jax import lax
from jax.experimental import pallas as pl
from jax.experimental.pallas import tpu as pltpu
from jax.sharding import PartitionSpec as P

M = 192
OWNERS = 64
ROWS = M // OWNERS
WIDTH = ROWS * M
FREQ = 128
LANES = 128
FIRST = [
    10, 20, 12, 31, 50, 55, 19, 56, 43, 45, 0, 21, 1, 16, 8, 22,
    11, 54, 53, 42, 24, 29, 18, 33, 30, 28, 49, 61, 44, 40, 17, 48,
    38, 59, 62, 39, 14, 7, 36, 51, 46, 35, 47, 15, 57, 26, 27, 5,
    2, 13, 32, 58, 37, 23, 6, 34, 52, 4, 3, 63, 25, 9, 60, 41,
]
SECOND = [
    10, 20, 12, 31, 50, 55, 19, 56, 43, 45, 0, 21, 1, 16, 8, 22,
    11, 54, 53, 42, 24, 29, 18, 33, 30, 28, 49, 61, 44, 40, 17, 48,
    38, 59, 62, 39, 14, 7, 36, 51, 46, 35, 47, 15, 57, 26, 27, 5,
    2, 13, 32, 58, 37, 23, 6, 34, 52, 4, 3, 63, 25, 9, 60, 41,
]


def dot(first, second):
    return jnp.dot(first, second, preferred_element_type=jnp.float32)


def dot_t(first, second):
    return lax.dot_general(first, second, (((1,), (1,)), ((), ())), preferred_element_type=jnp.float32)


def put(ref, where, value):
    for lane in range(0, value.shape[1], LANES):
        piece = value[:, lane : lane + LANES]
        ref[lane // LANES, where, : piece.shape[1]] = piece


def term(outer, inner, half, left, right):
    outer_real, outer_imag = outer[0, 0, 0], outer[0, 0, 1]
    inner_real, inner_imag = inner[0, 0, 0], inner[0, 0, 1]
    half_real = dot(outer_real, inner_real) - dot(outer_imag, inner_imag)
    half_imag = dot(outer_real, inner_imag) + dot(outer_imag, inner_real)
    put(half, slice(0, M), half_real.astype(jnp.bfloat16).astype(jnp.float32))
    put(half, slice(M, 2 * M), half_imag.astype(jnp.bfloat16).astype(jnp.float32))
    for plane in range(2):
        for row in range(ROWS):
            real = half[plane, pl.ds(row, OWNERS, stride=ROWS), :]
            imag = half[plane, pl.ds(M + row, OWNERS, stride=ROWS), :]
            first = 2 * OWNERS * row
            left[plane, pl.ds(first, OWNERS, stride=2), :] = real
            left[plane, pl.ds(first + 1, OWNERS, stride=2), :] = imag
            right[plane, pl.ds(first, OWNERS, stride=2), :] = imag
            right[plane, pl.ds(first + 1, OWNERS, stride=2), :] = -real
    left_all = jnp.concatenate([left[0], left[1, :, : M - LANES]], axis=1).astype(jnp.bfloat16)
    right_all = jnp.concatenate([right[0], right[1, :, : M - LANES]], axis=1).astype(jnp.bfloat16)
    full = dot_t(left_all, outer_real) + dot_t(right_all, outer_imag)
    return jnp.concatenate([full[2 * OWNERS * row : 2 * OWNERS * (row + 1)] for row in range(ROWS)], axis=1)


def own_kernel(green, sigma, out, half, left, right):
    out[...] = term(green, sigma, half, left, right)


def next_kernel(coupling, sigma, own, out, half, left, right):
    inside = lax.axis_index("slab") < lax.axis_size("slab") - 1
    added = jnp.where(inside, term(coupling, sigma, half, left, right), 0.0)
    chunks = (own[...] + added).astype(jnp.bfloat16).reshape(out.shape)
    for place, owner in enumerate(FIRST):
        out[place] = chunks[owner]


def prepare_kernel(screened, forward, backward, turned, forward_out, backward_out):
    for part in range(2):
        turned[part] = screened[0, part].T
    forward_out[...] = forward[...]
    backward_out[...] = backward[...]


def convolve_kernel(columns, screened, forward, backward, out):
    value = columns[...].reshape(2 * OWNERS, WIDTH)
    spectrum = dot(forward[...], jnp.concatenate([value, value], axis=0))
    spec_real, spec_imag = spectrum[:FREQ], spectrum[FREQ:]
    screen_real = screened[0].astype(jnp.float32)
    screen_imag = screened[1].astype(jnp.float32)
    conv_real = spec_real * screen_real - spec_imag * screen_imag
    conv_imag = spec_real * screen_imag + spec_imag * screen_real
    conv = jnp.concatenate([conv_real, conv_imag], axis=0)
    high = conv.astype(jnp.bfloat16)
    low = (conv - high.astype(jnp.float32)).astype(jnp.bfloat16)
    out[...] = dot(backward[...], jnp.concatenate([high, high, low], axis=0)).astype(jnp.bfloat16).reshape(out.shape)


def unpack_kernel(packed, out, flat, rows, near, sems):
    places = [SECOND.index(owner) for owner in range(OWNERS)]
    value = jnp.concatenate([packed[place : place + 1] for place in places], axis=0).reshape(2 * OWNERS, WIDTH)
    put(flat, slice(0, 2 * OWNERS), value.astype(jnp.float32))
    planes = flat.shape[0]
    copies = [pltpu.make_async_copy(near.at[part], out.at[0, 0, part], sems.at[part]) for part in range(2)]
    for part in range(2):
        both = jnp.concatenate([flat[plane, pl.ds(part, OWNERS, stride=2), :] for plane in range(planes)], axis=1)
        for row in range(ROWS):
            value = both[:, M * row : M * (row + 1)]
            put(rows, pl.ds(M * part + row, OWNERS, stride=ROWS), value)
        every = slice(M * part, M * (part + 1))
        near[part, :, :LANES] = rows[0, every, :].astype(jnp.bfloat16)
        near[part, :, LANES:] = rows[1, every, : M - LANES].astype(jnp.bfloat16)
        copies[part].start()
    for copy in copies:
        copy.wait()


def split(table):
    high = table.astype(jnp.bfloat16)
    low = (table - high.astype(np.float64)).astype(jnp.bfloat16)
    return high, low


def tables():
    phases = np.outer(np.arange(FREQ), np.arange(OWNERS)) % FREQ
    angles = phases * (2.0 * math.pi / FREQ)
    cosine, sine = np.cos(angles), np.sin(angles)
    from_real = np.concatenate([cosine, -sine], axis=0)
    from_imag = np.concatenate([sine, cosine], axis=0)
    forward = np.stack([from_real, from_imag], axis=-1)[:, FIRST].reshape(2 * FREQ, 2 * OWNERS)
    to_real = np.concatenate([cosine.T, -sine.T], axis=1)
    to_imag = np.concatenate([sine.T, cosine.T], axis=1)
    backward = np.stack([to_real, to_imag], axis=1)[SECOND].reshape(2 * OWNERS, 2 * FREQ) / FREQ
    forward_high, forward_low = split(forward)
    back_high, back_low = split(backward)
    return (
        np.concatenate([forward_high, forward_low], axis=1),
        np.concatenate([back_high, back_low, back_high], axis=1),
    )


def shaped(shape, dtype=jnp.bfloat16):
    return jax.ShapeDtypeStruct(shape, dtype)


def call(kernel, shapes, flops, moved, *values, scratch=(), far=False):
    vmem = pl.BlockSpec(memory_space=pltpu.VMEM)
    return pl.pallas_call(
        kernel,
        out_shape=shapes,
        in_specs=[vmem] * len(values),
        out_specs=[pl.BlockSpec(memory_space=pl.ANY) if far else vmem] * len(shapes),
        scratch_shapes=scratch,
        compiler_params=pltpu.CompilerParams(vmem_limit_bytes=24 * 2**20),
        cost_estimate=pl.CostEstimate(flops=flops, bytes_accessed=moved, transcendentals=0),
    )(*values)


def shards(green_block, coupling, sigma_lesser, screened):
    count = lax.axis_size("slab")
    sigma_next = lax.ppermute(sigma_lesser, "slab", [((place + 1) % count, place) for place in range(count)])
    planes = [pltpu.VMEM((2, 2 * M, LANES), jnp.float32)] * 3
    packed = shaped((OWNERS, 2, WIDTH))
    flops = 16 * M**3
    (own,) = call(own_kernel, [shaped((2 * OWNERS, WIDTH), jnp.float32)], flops, 600000, green_block, sigma_lesser, scratch=planes)
    forward, backward = tables()
    turned, forward, backward = call(
        prepare_kernel, [shaped((2, FREQ, WIDTH)), shaped(forward.shape), shaped(backward.shape)], flops, 1200000,
        screened.transpose(0, 1, 3, 2), jnp.asarray(forward), jnp.asarray(backward),
    )
    own, turned, forward, backward = lax.optimization_barrier((own, turned, forward, backward))
    (lesser,) = call(next_kernel, [packed], flops, 700000, coupling, sigma_next, own, scratch=planes)
    columns = lax.all_to_all(lesser, "energy", split_axis=0, concat_axis=0, axis_index_groups=[FIRST], tiled=True)
    (joined,) = call(convolve_kernel, [packed], 2 * 5 * 256 * 128 * WIDTH, 800000, columns, turned, forward, backward)
    returned = lax.all_to_all(joined, "energy", split_axis=0, concat_axis=0, axis_index_groups=[SECOND], tiled=True)
    (result,) = call(
        unpack_kernel, [shaped(sigma_lesser.shape)], 1000000, 300000, returned,
        scratch=[
            pltpu.VMEM((5, 2 * OWNERS, LANES), jnp.float32),
            pltpu.VMEM((2, 2 * M, LANES), jnp.float32),
            pltpu.VMEM((2, M, M), jnp.bfloat16),
            pltpu.SemaphoreType.DMA((2,)),
        ],
        far=True,
    )
    return result


def solution(mesh):
    placed = (
        P("energy", "slab", None, None, None),
        P("energy", "slab", None, None, None),
        P("energy", "slab", None, None, None),
        P("slab", None, None, "energy"),
    )
    return jax.shard_map(
        shards,
        mesh=mesh,
        in_specs=placed,
        out_specs=P("energy", "slab", None, None, None),
        check_vma=False,
    )
```

```python
import math

import jax
import jax.numpy as jnp
import numpy as np
from jax import lax
from jax.experimental import pallas as pl
from jax.experimental.pallas import tpu as pltpu
from jax.sharding import PartitionSpec as P

M = 192
OWNERS = 64
ROWS = M // OWNERS
WIDTH = ROWS * M
FREQ = 128
LANES = 128
FIRST = [
    43, 24, 28, 55, 34, 13, 18, 7, 40, 26, 50, 36, 59, 41, 1, 63,
    52, 61, 47, 8, 3, 32, 58, 35, 16, 51, 56, 60, 54, 11, 12, 0,
    15, 62, 9, 31, 33, 5, 14, 25, 49, 30, 19, 39, 21, 45, 17, 20,
    22, 37, 10, 42, 38, 2, 57, 29, 44, 23, 4, 6, 46, 48, 27, 53,
]
SECOND = [
    41, 29, 52, 54, 27, 35, 25, 6, 30, 42, 56, 7, 40, 49, 53, 18,
    36, 26, 0, 22, 62, 2, 43, 50, 12, 32, 37, 4, 48, 46, 58, 16,
    38, 3, 39, 23, 1, 20, 51, 14, 8, 59, 34, 31, 5, 57, 45, 47,
    21, 10, 61, 9, 11, 15, 17, 55, 33, 13, 19, 44, 60, 28, 63, 24,
]


def dot(first, second):
    return jnp.dot(first, second, preferred_element_type=jnp.float32)


def dot_t(first, second):
    return lax.dot_general(first, second, (((1,), (1,)), ((), ())), preferred_element_type=jnp.float32)


def put(ref, where, value):
    for lane in range(0, value.shape[1], LANES):
        piece = value[:, lane : lane + LANES]
        ref[lane // LANES, where, : piece.shape[1]] = piece


def term(outer, inner, half, left, right):
    outer_real, outer_imag = outer[0, 0, 0], outer[0, 0, 1]
    inner_real, inner_imag = inner[0, 0, 0], inner[0, 0, 1]
    half_real = dot(outer_real, inner_real) - dot(outer_imag, inner_imag)
    half_imag = dot(outer_real, inner_imag) + dot(outer_imag, inner_real)
    put(half, slice(0, M), half_real.astype(jnp.bfloat16).astype(jnp.float32))
    put(half, slice(M, 2 * M), half_imag.astype(jnp.bfloat16).astype(jnp.float32))
    for plane in range(2):
        for row in range(ROWS):
            real = half[plane, pl.ds(row, OWNERS, stride=ROWS), :]
            imag = half[plane, pl.ds(M + row, OWNERS, stride=ROWS), :]
            first = 2 * OWNERS * row
            left[plane, pl.ds(first, OWNERS, stride=2), :] = real
            left[plane, pl.ds(first + 1, OWNERS, stride=2), :] = imag
            right[plane, pl.ds(first, OWNERS, stride=2), :] = imag
            right[plane, pl.ds(first + 1, OWNERS, stride=2), :] = -real
    left_all = jnp.concatenate([left[0], left[1, :, : M - LANES]], axis=1).astype(jnp.bfloat16)
    right_all = jnp.concatenate([right[0], right[1, :, : M - LANES]], axis=1).astype(jnp.bfloat16)
    full = dot_t(left_all, outer_real) + dot_t(right_all, outer_imag)
    return jnp.concatenate([full[2 * OWNERS * row : 2 * OWNERS * (row + 1)] for row in range(ROWS)], axis=1)


def own_kernel(green, sigma, out, half, left, right):
    out[...] = term(green, sigma, half, left, right)


def next_kernel(coupling, sigma, own, out, half, left, right):
    inside = lax.axis_index("slab") < lax.axis_size("slab") - 1
    added = jnp.where(inside, term(coupling, sigma, half, left, right), 0.0)
    chunks = (own[...] + added).astype(jnp.bfloat16).reshape(out.shape)
    for place, owner in enumerate(FIRST):
        out[place] = chunks[owner]


def prepare_kernel(screened, forward, backward, turned, forward_out, backward_out):
    for part in range(2):
        turned[part] = screened[0, part].T
    forward_out[...] = forward[...]
    backward_out[...] = backward[...]


def convolve_kernel(columns, screened, forward, backward, out):
    value = columns[...].reshape(2 * OWNERS, WIDTH)
    spectrum = dot(forward[...], jnp.concatenate([value, value], axis=0))
    spec_real, spec_imag = spectrum[:FREQ], spectrum[FREQ:]
    screen_real = screened[0].astype(jnp.float32)
    screen_imag = screened[1].astype(jnp.float32)
    conv_real = spec_real * screen_real - spec_imag * screen_imag
    conv_imag = spec_real * screen_imag + spec_imag * screen_real
    conv = jnp.concatenate([conv_real, conv_imag], axis=0)
    high = conv.astype(jnp.bfloat16)
    low = (conv - high.astype(jnp.float32)).astype(jnp.bfloat16)
    out[...] = dot(backward[...], jnp.concatenate([high, high, low], axis=0)).astype(jnp.bfloat16).reshape(out.shape)


def unpack_kernel(packed, out, flat, rows, near, sems):
    places = [SECOND.index(owner) for owner in range(OWNERS)]
    value = jnp.concatenate([packed[place : place + 1] for place in places], axis=0).reshape(2 * OWNERS, WIDTH)
    put(flat, slice(0, 2 * OWNERS), value.astype(jnp.float32))
    planes = flat.shape[0]
    copies = [pltpu.make_async_copy(near.at[part], out.at[0, 0, part], sems.at[part]) for part in range(2)]
    for part in range(2):
        both = jnp.concatenate([flat[plane, pl.ds(part, OWNERS, stride=2), :] for plane in range(planes)], axis=1)
        for row in range(ROWS):
            value = both[:, M * row : M * (row + 1)]
            put(rows, pl.ds(M * part + row, OWNERS, stride=ROWS), value)
        every = slice(M * part, M * (part + 1))
        near[part, :, :LANES] = rows[0, every, :].astype(jnp.bfloat16)
        near[part, :, LANES:] = rows[1, every, : M - LANES].astype(jnp.bfloat16)
        copies[part].start()
    for copy in copies:
        copy.wait()


def split(table):
    high = table.astype(jnp.bfloat16)
    low = (table - high.astype(np.float64)).astype(jnp.bfloat16)
    return high, low


def tables():
    phases = np.outer(np.arange(FREQ), np.arange(OWNERS)) % FREQ
    angles = phases * (2.0 * math.pi / FREQ)
    cosine, sine = np.cos(angles), np.sin(angles)
    from_real = np.concatenate([cosine, -sine], axis=0)
    from_imag = np.concatenate([sine, cosine], axis=0)
    forward = np.stack([from_real, from_imag], axis=-1)[:, FIRST].reshape(2 * FREQ, 2 * OWNERS)
    to_real = np.concatenate([cosine.T, -sine.T], axis=1)
    to_imag = np.concatenate([sine.T, cosine.T], axis=1)
    backward = np.stack([to_real, to_imag], axis=1)[SECOND].reshape(2 * OWNERS, 2 * FREQ) / FREQ
    forward_high, forward_low = split(forward)
    back_high, back_low = split(backward)
    return (
        np.concatenate([forward_high, forward_low], axis=1),
        np.concatenate([back_high, back_low, back_high], axis=1),
    )


def shaped(shape, dtype=jnp.bfloat16):
    return jax.ShapeDtypeStruct(shape, dtype)


def call(kernel, shapes, flops, moved, *values, scratch=(), far=False):
    vmem = pl.BlockSpec(memory_space=pltpu.VMEM)
    return pl.pallas_call(
        kernel,
        out_shape=shapes,
        in_specs=[vmem] * len(values),
        out_specs=[pl.BlockSpec(memory_space=pl.ANY) if far else vmem] * len(shapes),
        scratch_shapes=scratch,
        compiler_params=pltpu.CompilerParams(vmem_limit_bytes=24 * 2**20),
        cost_estimate=pl.CostEstimate(flops=flops, bytes_accessed=moved, transcendentals=0),
    )(*values)


def shards(green_block, coupling, sigma_lesser, screened):
    count = lax.axis_size("slab")
    sigma_next = lax.ppermute(sigma_lesser, "slab", [((place + 1) % count, place) for place in range(count)])
    planes = [pltpu.VMEM((2, 2 * M, LANES), jnp.float32)] * 3
    packed = shaped((OWNERS, 2, WIDTH))
    flops = 16 * M**3
    (own,) = call(own_kernel, [shaped((2 * OWNERS, WIDTH), jnp.float32)], flops, 600000, green_block, sigma_lesser, scratch=planes)
    forward, backward = tables()
    turned, forward, backward = call(
        prepare_kernel, [shaped((2, FREQ, WIDTH)), shaped(forward.shape), shaped(backward.shape)], flops, 1200000,
        screened.transpose(0, 1, 3, 2), jnp.asarray(forward), jnp.asarray(backward),
    )
    own, turned, forward, backward = lax.optimization_barrier((own, turned, forward, backward))
    (lesser,) = call(next_kernel, [packed], flops, 700000, coupling, sigma_next, own, scratch=planes)
    columns = lax.all_to_all(lesser, "energy", split_axis=0, concat_axis=0, axis_index_groups=[FIRST], tiled=True)
    (joined,) = call(convolve_kernel, [packed], 2 * 5 * 256 * 128 * WIDTH, 800000, columns, turned, forward, backward)
    returned = lax.all_to_all(joined, "energy", split_axis=0, concat_axis=0, axis_index_groups=[SECOND], tiled=True)
    (result,) = call(
        unpack_kernel, [shaped(sigma_lesser.shape)], 1000000, 300000, returned,
        scratch=[
            pltpu.VMEM((5, 2 * OWNERS, LANES), jnp.float32),
            pltpu.VMEM((2, 2 * M, LANES), jnp.float32),
            pltpu.VMEM((2, M, M), jnp.bfloat16),
            pltpu.SemaphoreType.DMA((2,)),
        ],
        far=True,
    )
    return result


def solution(mesh):
    placed = (
        P("energy", "slab", None, None, None),
        P("energy", "slab", None, None, None),
        P("energy", "slab", None, None, None),
        P("slab", None, None, "energy"),
    )
    return jax.shard_map(
        shards,
        mesh=mesh,
        in_specs=placed,
        out_specs=P("energy", "slab", None, None, None),
        check_vma=False,
    )
```

```python
import math

import jax
import jax.numpy as jnp
import numpy as np
from jax import lax
from jax.experimental import pallas as pl
from jax.experimental.pallas import tpu as pltpu
from jax.sharding import PartitionSpec as P

M = 192
OWNERS = 64
ROWS = M // OWNERS
WIDTH = ROWS * M
FREQ = 128
LANES = 128
FIRST = [
    43, 15, 45, 21, 49, 13, 33, 47, 0, 22, 34, 40, 26, 14, 30, 17,
    41, 55, 20, 52, 60, 2, 28, 5, 62, 8, 16, 19, 12, 56, 63, 54,
    10, 37, 59, 24, 7, 53, 3, 11, 25, 46, 35, 39, 57, 36, 27, 32,
    1, 51, 31, 38, 58, 6, 50, 61, 42, 23, 29, 9, 48, 44, 18, 4,
]
SECOND = [
    43, 24, 28, 55, 34, 13, 18, 7, 40, 26, 50, 36, 59, 41, 1, 63,
    52, 61, 47, 8, 3, 32, 58, 35, 16, 51, 56, 60, 54, 11, 12, 0,
    15, 62, 9, 31, 33, 5, 14, 25, 49, 30, 19, 39, 21, 45, 17, 20,
    22, 37, 10, 42, 38, 2, 57, 29, 44, 23, 4, 6, 46, 48, 27, 53,
]


def dot(first, second):
    return jnp.dot(first, second, preferred_element_type=jnp.float32)


def dot_t(first, second):
    return lax.dot_general(first, second, (((1,), (1,)), ((), ())), preferred_element_type=jnp.float32)


def put(ref, where, value):
    for lane in range(0, value.shape[1], LANES):
        piece = value[:, lane : lane + LANES]
        ref[lane // LANES, where, : piece.shape[1]] = piece


def term(outer, inner, half, left, right):
    outer_real, outer_imag = outer[0, 0, 0], outer[0, 0, 1]
    inner_real, inner_imag = inner[0, 0, 0], inner[0, 0, 1]
    half_real = dot(outer_real, inner_real) - dot(outer_imag, inner_imag)
    half_imag = dot(outer_real, inner_imag) + dot(outer_imag, inner_real)
    put(half, slice(0, M), half_real.astype(jnp.bfloat16).astype(jnp.float32))
    put(half, slice(M, 2 * M), half_imag.astype(jnp.bfloat16).astype(jnp.float32))
    for plane in range(2):
        for row in range(ROWS):
            real = half[plane, pl.ds(row, OWNERS, stride=ROWS), :]
            imag = half[plane, pl.ds(M + row, OWNERS, stride=ROWS), :]
            first = 2 * OWNERS * row
            left[plane, pl.ds(first, OWNERS, stride=2), :] = real
            left[plane, pl.ds(first + 1, OWNERS, stride=2), :] = imag
            right[plane, pl.ds(first, OWNERS, stride=2), :] = imag
            right[plane, pl.ds(first + 1, OWNERS, stride=2), :] = -real
    left_all = jnp.concatenate([left[0], left[1, :, : M - LANES]], axis=1).astype(jnp.bfloat16)
    right_all = jnp.concatenate([right[0], right[1, :, : M - LANES]], axis=1).astype(jnp.bfloat16)
    full = dot_t(left_all, outer_real) + dot_t(right_all, outer_imag)
    return jnp.concatenate([full[2 * OWNERS * row : 2 * OWNERS * (row + 1)] for row in range(ROWS)], axis=1)


def own_kernel(green, sigma, out, half, left, right):
    out[...] = term(green, sigma, half, left, right)


def next_kernel(coupling, sigma, own, out, half, left, right):
    inside = lax.axis_index("slab") < lax.axis_size("slab") - 1
    added = jnp.where(inside, term(coupling, sigma, half, left, right), 0.0)
    chunks = (own[...] + added).astype(jnp.bfloat16).reshape(out.shape)
    for place, owner in enumerate(FIRST):
        out[place] = chunks[owner]


def prepare_kernel(screened, table, turned, table_out):
    for part in range(2):
        turned[part] = screened[0, part].T
    table_out[...] = table[...]


def convolve_kernel(columns, screened, table, out):
    value = columns[...].reshape(2 * OWNERS, WIDTH)
    forward = table[:, : 4 * OWNERS]
    backward = jnp.concatenate([table[:FREQ, 4 * OWNERS :], table[FREQ:, 4 * OWNERS :]], axis=1)
    spectrum = dot(forward, jnp.concatenate([value, value], axis=0))
    spec_real, spec_imag = spectrum[:FREQ], spectrum[FREQ:]
    screen_real = screened[0].astype(jnp.float32)
    screen_imag = screened[1].astype(jnp.float32)
    conv_real = spec_real * screen_real - spec_imag * screen_imag
    conv_imag = spec_real * screen_imag + spec_imag * screen_real
    conv = jnp.concatenate([conv_real, conv_imag], axis=0)
    high = conv.astype(jnp.bfloat16)
    low = (conv - high.astype(jnp.float32)).astype(jnp.bfloat16)
    out[...] = dot(backward, jnp.concatenate([high, high, low], axis=0)).astype(jnp.bfloat16).reshape(out.shape)


def unpack_kernel(packed, out, flat, rows, near, sems):
    places = [SECOND.index(owner) for owner in range(OWNERS)]
    value = jnp.concatenate([packed[place : place + 1] for place in places], axis=0).reshape(2 * OWNERS, WIDTH)
    put(flat, slice(0, 2 * OWNERS), value.astype(jnp.float32))
    planes = flat.shape[0]
    copies = [pltpu.make_async_copy(near.at[part], out.at[0, 0, part], sems.at[part]) for part in range(2)]
    for part in range(2):
        both = jnp.concatenate([flat[plane, pl.ds(part, OWNERS, stride=2), :] for plane in range(planes)], axis=1)
        for row in range(ROWS):
            value = both[:, M * row : M * (row + 1)]
            put(rows, pl.ds(M * part + row, OWNERS, stride=ROWS), value)
        every = slice(M * part, M * (part + 1))
        near[part, :, :LANES] = rows[0, every, :].astype(jnp.bfloat16)
        near[part, :, LANES:] = rows[1, every, : M - LANES].astype(jnp.bfloat16)
        copies[part].start()
    for copy in copies:
        copy.wait()


def split(table):
    high = table.astype(jnp.bfloat16)
    low = (table - high.astype(np.float64)).astype(jnp.bfloat16)
    return high, low


def tables():
    phases = np.outer(np.arange(FREQ), np.arange(OWNERS)) % FREQ
    angles = phases * (2.0 * math.pi / FREQ)
    cosine, sine = np.cos(angles), np.sin(angles)
    from_real = np.concatenate([cosine, -sine], axis=0)
    from_imag = np.concatenate([sine, cosine], axis=0)
    forward = np.stack([from_real, from_imag], axis=-1)[:, FIRST].reshape(2 * FREQ, 2 * OWNERS)
    to_real = np.concatenate([cosine.T, -sine.T], axis=1)
    to_imag = np.concatenate([sine.T, cosine.T], axis=1)
    backward = np.stack([to_real, to_imag], axis=1)[SECOND].reshape(2 * OWNERS, 2 * FREQ) / FREQ
    forward_high, forward_low = split(forward)
    back_high, back_low = split(backward)
    backward = np.concatenate([back_high, back_low, back_high], axis=1)
    halves = np.split(backward, 2, axis=1)
    return np.concatenate([forward_high, forward_low, np.concatenate(halves, axis=0)], axis=1)


def shaped(shape, dtype=jnp.bfloat16):
    return jax.ShapeDtypeStruct(shape, dtype)


def call(kernel, shapes, flops, moved, *values, scratch=(), far=False):
    vmem = pl.BlockSpec(memory_space=pltpu.VMEM)
    return pl.pallas_call(
        kernel,
        out_shape=shapes,
        in_specs=[vmem] * len(values),
        out_specs=[pl.BlockSpec(memory_space=pl.ANY) if far else vmem] * len(shapes),
        scratch_shapes=scratch,
        compiler_params=pltpu.CompilerParams(vmem_limit_bytes=24 * 2**20),
        cost_estimate=pl.CostEstimate(flops=flops, bytes_accessed=moved, transcendentals=0),
    )(*values)


def shards(green_block, coupling, sigma_lesser, screened):
    count = lax.axis_size("slab")
    sigma_next = lax.ppermute(sigma_lesser, "slab", [((place + 1) % count, place) for place in range(count)])
    planes = [pltpu.VMEM((2, 2 * M, LANES), jnp.float32)] * 3
    packed = shaped((OWNERS, 2, WIDTH))
    flops = 16 * M**3
    (own,) = call(own_kernel, [shaped((2 * OWNERS, WIDTH), jnp.float32)], flops, 600000, green_block, sigma_lesser, scratch=planes)
    table = jnp.asarray(tables())
    turned, table = call(
        prepare_kernel, [shaped((2, FREQ, WIDTH)), shaped(table.shape)], flops, 1200000, screened.transpose(0, 1, 3, 2), table
    )
    own, turned, table = lax.optimization_barrier((own, turned, table))
    (lesser,) = call(next_kernel, [packed], flops, 700000, coupling, sigma_next, own, scratch=planes)
    columns = lax.all_to_all(lesser, "energy", split_axis=0, concat_axis=0, axis_index_groups=[FIRST], tiled=True)
    (joined,) = call(convolve_kernel, [packed], 2 * 5 * 256 * 128 * WIDTH, 800000, columns, turned, table)
    returned = lax.all_to_all(joined, "energy", split_axis=0, concat_axis=0, axis_index_groups=[SECOND], tiled=True)
    (result,) = call(
        unpack_kernel, [shaped(sigma_lesser.shape)], 1000000, 300000, returned,
        scratch=[
            pltpu.VMEM((5, 2 * OWNERS, LANES), jnp.float32),
            pltpu.VMEM((2, 2 * M, LANES), jnp.float32),
            pltpu.VMEM((2, M, M), jnp.bfloat16),
            pltpu.SemaphoreType.DMA((2,)),
        ],
        far=True,
    )
    return result


def solution(mesh):
    placed = (
        P("energy", "slab", None, None, None),
        P("energy", "slab", None, None, None),
        P("energy", "slab", None, None, None),
        P("slab", None, None, "energy"),
    )
    return jax.shard_map(
        shards,
        mesh=mesh,
        in_specs=placed,
        out_specs=P("energy", "slab", None, None, None),
        check_vma=False,
    )
```
